512 devices in a mesh: frame: 64 (over y, x, core), head: 8 (over z).
Axes of the slice: x: 4, y: 8, z: 8, core: 2. Of those that a mesh axis runs over, the one named last changes fastest.
Arguments:
- queries: bfloat16 [16384, 3072], P('frame', 'head')
- keys: bfloat16 [16384, 3072], P('frame', 'head')
- values: bfloat16 [16384, 3072], P('frame', 'head'), may hold values from -6 to 6
- text_keys: bfloat16 [256, 3072], P('frame', 'head'), may hold values from -6 to 6
- text_values: bfloat16 [256, 3072], P('frame', 'head'), may hold values from -6 to 6
- head_kinds: int32 [24], replicated, may hold values 0 or 1
- text_count: int32 [1], replicated, may hold values from 64 to 256
- w_out: bfloat16 [3072, 3072], P('head', 'frame'), may hold values from -0.109375 to 0.109375
Outputs:
- projected: bfloat16 [16384, 3072], P(('frame', 'head'))
The draws below stay inside these ranges and needn't reach their ends.
All inputs are finite; a program needn't handle non-finite values.
Results may differ from the reference program's by a relative error of at most 0.022.
Values may be sent and summed in bfloat16 or wider, within the bound.
A program may use at most 64 MiB of HBM per device.

```python
import jax
import jax.numpy as jnp
from jax import lax

HEADS = 24
HD = 128
D = 3072
TEXT = 256
TOK = 256
FRAMES = 64
ROWS = 16384
HG = 3
N_HEAD = 8


def draw_queries(key, part):
    key = jax.random.fold_in(key, 11)
    base = jax.random.normal(key, (ROWS, HEADS * HD), jnp.float32)
    return base.astype(jnp.bfloat16)


def draw_keys(key, part):
    key = jax.random.fold_in(key, 23)
    base = jax.random.normal(key, (ROWS, HEADS * HD), jnp.float32)
    return base.astype(jnp.bfloat16)


def set_ends(drawn, stream_key, low, top_value):
    shape = drawn.shape
    index_at = [jax.random.randint(jax.random.fold_in(stream_key, axis), (), 0, shape[axis]) for axis in range(len(shape))]
    drawn = drawn.at[tuple(index_at)].set(low)
    longest = shape.index(max(shape))
    index_at[longest] = (index_at[longest] + 1) % shape[longest]
    return drawn.at[tuple(index_at)].set(top_value)


def level_of(key, dims, split, smallest, top_value):
    def one(axis_at, shards_of):
        steps = jax.random.uniform(jax.random.fold_in(jax.random.fold_in(key, 6), axis_at), (shards_of,), jnp.float32, smallest / len(split), top_value / len(split))
        return jnp.repeat(jnp.exp(steps), dims[axis_at] // shards_of).reshape((-1,) + (1,) * (len(dims) - axis_at - 1))

    level = one(*split[0])
    for cut in split[1:]:
        level = level * one(*cut)
    return level


def noise(key, shape, deviation, most, pieces=(), held_as=jnp.bfloat16):
    values = jax.random.normal(key, shape, jnp.float32) * deviation
    if len(pieces) > 0:
        values = level_of(key, shape, pieces, -0.22, 0.18) * values
    return jnp.clip(values, min=-most, max=most).astype(held_as)


def setup_inputs(seed: int = 0) -> dict:
    arg_keys = jax.random.split(jax.random.key(seed), 9)
    return {
        "queries": draw_queries(jax.random.fold_in(arg_keys[8], 71), 0),
        "keys": draw_keys(jax.random.fold_in(arg_keys[8], 71), 0),
        "values": noise(arg_keys[2], (ROWS, HEADS * HD), 1.0, 6.0, ((0, 64), (1, 8))),
        "text_keys": noise(arg_keys[3], (TEXT, HEADS * HD), 1.0, 6.0, ((0, 64), (1, 8))),
        "text_values": noise(arg_keys[4], (TEXT, HEADS * HD), 1.0, 6.0, ((0, 64), (1, 8))),
        "head_kinds": set_ends((jax.random.randint(arg_keys[5], (HEADS,), 0, 2) < 1).astype(jnp.int32), jax.random.fold_in(arg_keys[5], 1), 0, 1),
        "text_count": jax.random.randint(arg_keys[6], (1,), TEXT // 4, TEXT + 1).astype(jnp.int32),
        "w_out": noise(arg_keys[7], (HEADS * HD, D), (HEADS * HD) ** -0.5, 0.109375, ((0, 8), (1, 64))),
    }


def soft_weights(scores):
    top = jnp.max(scores, axis=-1, keepdims=True)
    expo = jnp.exp(scores - top)
    return (expo / jnp.sum(expo, axis=-1, keepdims=True)).astype(jnp.bfloat16)


def reference(queries, keys, values, text_keys, text_values, head_kinds, text_count, w_out):
    scale = HD ** -0.5
    q_all = queries.reshape(FRAMES, TOK, HEADS, HD)
    k_all = keys.reshape(FRAMES, TOK, HEADS, HD)
    v_all = values.reshape(FRAMES, TOK, HEADS, HD)
    text_k = text_keys.reshape(TEXT, HEADS, HD)
    text_v = text_values.reshape(TEXT, HEADS, HD)
    live = jnp.arange(TOK + TEXT, dtype=jnp.int32) < TOK + text_count[0]

    def spatial_frame(frame_parts):
        query, key_frame, value_frame = frame_parts
        key_all = jnp.concatenate([key_frame, text_k], axis=0)
        value_all = jnp.concatenate([value_frame, text_v], axis=0)
        scores = jnp.einsum("qhd,khd->hqk", query.astype(jnp.float32), key_all.astype(jnp.float32)) * scale
        scores = jnp.where(live[None, None, :], scores, -1e30)
        weights = soft_weights(scores)
        return jnp.einsum("hqk,khd->qhd", weights.astype(jnp.float32), value_all.astype(jnp.float32))

    spatial = lax.map(spatial_frame, (q_all, k_all, v_all))

    def temporal_head(head_parts):
        query, key_head, value_head = head_parts
        scores = jnp.einsum("fpd,gpd->pfg", query.astype(jnp.float32), key_head.astype(jnp.float32)) * scale
        weights = soft_weights(scores)
        return jnp.einsum("pfg,gpd->fpd", weights.astype(jnp.float32), value_head.astype(jnp.float32))

    moved = (jnp.moveaxis(q_all, 2, 0), jnp.moveaxis(k_all, 2, 0), jnp.moveaxis(v_all, 2, 0))
    temporal = jnp.moveaxis(lax.map(temporal_head, moved), 0, 2)
    choose = (head_kinds == 1)[None, None, :, None]
    mixed = jnp.where(choose, temporal, spatial).astype(jnp.bfloat16).reshape(ROWS, HEADS * HD)
    grouped = mixed.reshape(ROWS, N_HEAD, HG * HD)
    w_grouped = w_out.reshape(N_HEAD, HG * HD, D)

    def add_group(total, index):
        cols = lax.dynamic_index_in_dim(grouped, index, 1, keepdims=False)
        rows = lax.dynamic_index_in_dim(w_grouped, index, 0, keepdims=False)
        term = jnp.dot(cols, rows, preferred_element_type=jnp.float32).astype(jnp.bfloat16)
        return total + term.astype(jnp.float32), None

    total, _ = lax.scan(add_group, jnp.zeros((ROWS, D), jnp.float32), jnp.arange(N_HEAD, dtype=jnp.int32))
    return total.astype(jnp.bfloat16)
```

```python
import functools

import jax
import jax.numpy as jnp
from jax import lax
from jax.experimental import pallas as pl
from jax.experimental.pallas import tpu as pltpu
from jax.sharding import PartitionSpec as P

HD = 128
MESH = pl.DeviceIdType.MESH
F32 = jnp.float32
BF16 = jnp.bfloat16
NT = (((1,), (1,)), ((), ()))
NN = (((1,), (0,)), ((), ()))
SCALE = HD ** (-0.5)
FAR_FIRST = (4, 3, 5, 2, 6, 1, 7)


def dot(a, b, dims=NN):
    return lax.dot_general(a, b, dims, preferred_element_type=F32)


def send(src, dst, send_sem, recv_sem, **where):
    copy = pltpu.make_async_remote_copy(
        src_ref=src, dst_ref=dst, send_sem=send_sem, recv_sem=recv_sem,
        device_id=where, device_id_type=MESH,
    )
    copy.start()


def wait_for(ref, sem):
    pltpu.make_async_copy(ref, ref, sem).wait()


def swap_matrix():
    out = lax.broadcasted_iota(jnp.int32, (256, 256), 0)
    src = lax.broadcasted_iota(jnp.int32, (256, 256), 1)
    want = ((out // 4) % 8) * 32 + (out // 32) * 4 + out % 4
    return jnp.where(src == want, 1.0, 0.0).astype(BF16)


def text_matrix():
    out = lax.broadcasted_iota(jnp.int32, (64, 128), 0)
    src = lax.broadcasted_iota(jnp.int32, (64, 128), 1)
    want = ((out % 32) // 4) * 16 + (out // 32) * 4 + out % 4
    return jnp.where(src == want, 1.0, 0.0).astype(BF16)


def kernel(
    q_ref, k_ref, v_ref, slot_ref, kinds_ref, count_ref, out_ref,
    rx, sy, ty, oy, uy, sx, vx, wg, tk, tv, spat, mixed, part, rsend, rrecv,
    fx_s, fx_r, fy_s, fy_r, by_s, by_r, bx_s, bx_r,
    gy_s, gy_r, gx_s, gx_r, gp_s, gp_r, rs_s, rs_r,
):
    frame = lax.axis_index("frame")
    z = lax.axis_index("head")
    y = frame // 8
    j = frame % 8
    x = j // 2
    core = j % 2

    def at(yy, jj):
        return yy * 8 + jj

    def turn(base, step, size):
        return (base + step + size) % size

    j_right = turn(x, 1, 4) * 2 + core
    j_left = turn(x, -1, 4) * 2 + core
    j_far = turn(x, 2, 4) * 2 + core
    partner = at(y, x * 2 + 1 - core)

    barrier = pltpu.get_barrier_semaphore()
    for k in range(1, 8):
        pl.semaphore_signal(barrier, inc=1, device_id={"frame": at(turn(y, k, 8), j)}, device_id_type=MESH)
        pl.semaphore_signal(barrier, inc=1, device_id={"frame": at(y, turn(j, k, 8))}, device_id_type=MESH)
    for k in (1, -1):
        pl.semaphore_signal(barrier, inc=1, device_id={"head": turn(z, k, 8)}, device_id_type=MESH)
    pl.semaphore_wait(barrier, 16)

    def rows(block):
        return pl.ds(pl.multiple_of(block * 32, 32), 32)

    ins = (q_ref, k_ref, v_ref)
    for i in range(3):
        for k in FAR_FIRST:
            jj = turn(j, k, 8)
            send(ins[i].at[rows(jj)], rx.at[i, j], fx_s.at[i], fx_r.at[i], frame=at(y, jj))
        rx[i, j] = ins[i][rows(j), :]

    wg[y, j] = slot_ref[...]

    def gather_y(step):
        up = turn(y, 1 - step, 8)
        down = turn(y, step - 1, 8)
        cut_up = pl.ds(0, 32) if step == 4 else pl.ds(0, 64)
        cut_down = pl.ds(32, 32) if step == 4 else pl.ds(0, 64)
        src = wg.at[up, j, cut_up]
        send(src, src, gy_s.at[0, step - 1], gy_r.at[0, step - 1], frame=at(turn(y, 1, 8), j))
        src = wg.at[down, j, cut_down]
        send(src, src, gy_s.at[1, step - 1], gy_r.at[1, step - 1], frame=at(turn(y, -1, 8), j))

    def gathered_y(step):
        cut_up = pl.ds(0, 32) if step == 4 else pl.ds(0, 64)
        cut_down = pl.ds(32, 32) if step == 4 else pl.ds(0, 64)
        wait_for(wg.at[turn(y, -step, 8), j, cut_up], gy_r.at[0, step - 1])
        wait_for(wg.at[turn(y, step, 8), j, cut_down], gy_r.at[1, step - 1])

    gather_y(1)
    swap = swap_matrix()

    def turn_over(i):
        wait_for(rx.at[i, pl.ds(0, 7)], fx_r.at[i])
        sy[i] = dot(swap, rx[i].reshape(256, 384)).astype(BF16).reshape(8, 32, 384)
        for k in FAR_FIRST:
            yy = turn(y, k, 8)
            send(sy.at[i, yy], ty.at[i, y], fy_s.at[i], fy_r.at[i], frame=at(yy, j))
        ty[i, y] = sy[i, y]

    turn_over(0)
    gathered_y(1)
    gather_y(2)
    turn_over(1)
    gathered_y(2)
    gather_y(3)
    turn_over(2)
    gathered_y(3)
    gather_y(4)
    gathered_y(4)

    def block(jj):
        return wg.at[pl.ds(0, 8), jj]

    def low(jj):
        return wg.at[pl.ds(0, 4), jj]

    def high(jj):
        return wg.at[pl.ds(4, 4), jj]

    send(block(j), block(j), gx_s.at[0, 0], gx_r.at[0, 0], frame=at(y, j_right))
    send(block(j), block(j), gx_s.at[1, 0], gx_r.at[1, 0], frame=at(y, j_left))
    send(block(j), block(j), gp_s.at[0], gp_r.at[0], frame=partner)

    row = lax.broadcasted_iota(jnp.int32, (256, 256), 0)
    col = lax.broadcasted_iota(jnp.int32, (256, 256), 1)
    same = (row % 4) == (col % 4)
    for i in range(3):
        wait_for(ty.at[i, pl.ds(0, 7)], fy_r.at[i])
    for h in range(3):
        lanes = pl.ds(h * HD, HD)
        qh = ty[0, :, :, lanes].reshape(256, HD)
        kh = ty[1, :, :, lanes].reshape(256, HD)
        vh = ty[2, :, :, lanes].reshape(256, HD)
        scores = jnp.where(same, dot(qh, kh, NT) * SCALE, -1e30)
        expo = jnp.exp(scores - jnp.max(scores, axis=1, keepdims=True))
        total = jnp.sum(expo, axis=1, keepdims=True)
        oy[h] = (dot(expo.astype(BF16), vh) / total).astype(BF16).reshape(8, 32, HD)
        for k in FAR_FIRST:
            yy = turn(y, k, 8)
            send(oy.at[h, yy], uy.at[h, y], by_s.at[h], by_r.at[h], frame=at(yy, j))
        uy[h, y] = oy[h, y]

    wait_for(block(j_left), gx_r.at[0, 0])
    send(low(j_left), low(j_left), gx_s.at[0, 1], gx_r.at[0, 1], frame=at(y, j_right))
    send(block(j_left), block(j_left), gp_s.at[1], gp_r.at[1], frame=partner)
    wait_for(block(j_right), gx_r.at[1, 0])
    send(high(j_right), high(j_right), gx_s.at[1, 1], gx_r.at[1, 1], frame=at(y, j_left))
    send(block(j_right), block(j_right), gp_s.at[2], gp_r.at[2], frame=partner)
    wait_for(low(j_far), gx_r.at[0, 1])
    wait_for(high(j_far), gx_r.at[1, 1])
    send(block(j_far), block(j_far), gp_s.at[3], gp_r.at[3], frame=partner)

    for h in range(3):
        wait_for(uy.at[h, pl.ds(0, 7)], by_r.at[h])
        sx[h] = dot(swap, uy[h].reshape(256, HD)).astype(BF16).reshape(8, 32, HD)
        for k in FAR_FIRST:
            jj = turn(j, k, 8)
            send(sx.at[h, jj], vx.at[h, j], bx_s.at[h], bx_r.at[h], frame=at(y, jj))
        vx[h, j] = sx[h, j]

    shift = 1 - 2 * core
    for i, jj in enumerate((j, j_left, j_right, j_far)):
        wait_for(block(jj + shift), gp_r.at[i])

    pick = text_matrix()
    for b in range(8):
        both = dot(pick, wg[b, :, 48:64, :].reshape(128, 384)).astype(BF16)
        tk[b * 32:(b + 1) * 32, :] = both[:32]
        tv[b * 32:(b + 1) * 32, :] = both[32:]
    live = col < count_ref[0]
    for h in range(3):
        lanes = pl.ds(h * HD, HD)
        qh = q_ref[:, lanes]
        own = dot(qh, k_ref[:, lanes], NT) * SCALE
        text = jnp.where(live, dot(qh, tk[:, lanes], NT) * SCALE, -1e30)
        top = jnp.maximum(
            jnp.max(own, axis=1, keepdims=True), jnp.max(text, axis=1, keepdims=True)
        )
        e_own = jnp.exp(own - top)
        e_text = jnp.exp(text - top)
        total = jnp.sum(e_own, axis=1, keepdims=True) + jnp.sum(e_text, axis=1, keepdims=True)
        result = dot(e_own.astype(BF16), v_ref[:, lanes]) + dot(e_text.astype(BF16), tv[:, lanes])
        spat[:, lanes] = (result / total).astype(BF16)

    for h in range(3):
        lanes = pl.ds(h * HD, HD)
        wait_for(vx.at[h, pl.ds(0, 7)], bx_r.at[h])
        temporal = vx[h].reshape(256, HD)
        mixed[:, lanes] = jnp.where(kinds_ref[z * 3 + h] == 1, temporal, spat[:, lanes])

    ahead = turn(z, 1, 8)
    behind = turn(z, -1, 8)
    length = lambda b, way: 4 if (b + way) % 2 == 0 else 3

    def dest(b, way, stage):
        left = length(b, way) - stage
        return turn(z, left if way == 0 else -left, 8)

    def pass_on(src, b, way, stage):
        send(src, rrecv.at[way, b, stage], rs_s.at[way, b, stage], rs_r.at[way, b, stage],
             head=ahead if way == 0 else behind)

    for b in range(8):
        term = dot(mixed[...], wg[b, :, 0:48, :].reshape(384, 384), NT)
        part[b] = term.astype(BF16).reshape(8, 32, 384)
        for way in range(2):
            pass_on(part.at[b, dest(b, way, 0)], b, way, 0)
    for stage in range(1, 4):
        for b in range(8):
            for way in range(2):
                if stage < length(b, way):
                    wait_for(rrecv.at[way, b, stage - 1], rs_r.at[way, b, stage - 1])
                    own = part[b, dest(b, way, stage)].astype(F32)
                    rsend[way, b, stage] = (own + rrecv[way, b, stage - 1].astype(F32)).astype(BF16)
                    pass_on(rsend.at[way, b, stage], b, way, stage)
    for b in range(8):
        own = part[b, z].astype(F32)
        for way in range(2):
            last = length(b, way) - 1
            wait_for(rrecv.at[way, b, last], rs_r.at[way, b, last])
            own = own + rrecv[way, b, last].astype(F32)
        out_ref[:, b * 384:(b + 1) * 384] = own.astype(BF16)

    for i in range(3):
        wait_for(rx.at[i, pl.ds(0, 7)], fx_s.at[i])
        wait_for(sy.at[i, pl.ds(0, 7)], fy_s.at[i])
        wait_for(oy.at[i, pl.ds(0, 7)], by_s.at[i])
        wait_for(sx.at[i, pl.ds(0, 7)], bx_s.at[i])
    for way in range(2):
        for step in range(4):
            cut = pl.ds(0, 32) if step == 3 else pl.ds(0, 64)
            wait_for(wg.at[0, 0, cut], gy_s.at[way, step])
        wait_for(block(0), gx_s.at[way, 0])
        wait_for(low(0), gx_s.at[way, 1])
        for b in range(8):
            for stage in range(length(b, way)):
                wait_for(rsend.at[way, b, stage], rs_s.at[way, b, stage])
    for i in range(4):
        wait_for(block(0), gp_s.at[i])


def per_device(queries, keys, values, text_keys, text_values, head_kinds, text_count, w_out):
    slot = jnp.concatenate(
        [w_out.T, text_keys, text_values, jnp.zeros((8, w_out.shape[0]), BF16)], axis=0
    )
    vmem = pl.BlockSpec(memory_space=pltpu.VMEM)
    smem = pl.BlockSpec(memory_space=pltpu.SMEM)
    dma = pltpu.SemaphoreType.DMA
    return pl.pallas_call(
        kernel,
        out_shape=jax.ShapeDtypeStruct((32, 3072), BF16),
        in_specs=[vmem] * 4 + [smem] * 2,
        out_specs=vmem,
        scratch_shapes=[
            pltpu.VMEM((3, 8, 32, 384), BF16),
            pltpu.VMEM((3, 8, 32, 384), BF16),
            pltpu.VMEM((3, 8, 32, 384), BF16),
            pltpu.VMEM((3, 8, 32, HD), BF16),
            pltpu.VMEM((3, 8, 32, HD), BF16),
            pltpu.VMEM((3, 8, 32, HD), BF16),
            pltpu.VMEM((3, 8, 32, HD), BF16),
            pltpu.VMEM((8, 8, 64, 384), BF16),
            pltpu.VMEM((256, 384), BF16),
            pltpu.VMEM((256, 384), BF16),
            pltpu.VMEM((256, 384), BF16),
            pltpu.VMEM((256, 384), BF16),
            pltpu.VMEM((8, 8, 32, 384), BF16),
            pltpu.VMEM((2, 8, 4, 32, 384), BF16),
            pltpu.VMEM((2, 8, 4, 32, 384), BF16),
        ]
        + [dma((3,))] * 8
        + [dma((2, 4))] * 2
        + [dma((2, 2))] * 2
        + [dma((4,))] * 2
        + [dma((2, 8, 4))] * 2,
        compiler_params=pltpu.CompilerParams(
            collective_id=0, has_side_effects=True, vmem_limit_bytes=40 * 1024 * 1024
        ),
    )(queries, keys, values, slot, head_kinds, text_count)


def solution(mesh):
    in_specs = (
        P("frame", "head"),
        P("frame", "head"),
        P("frame", "head"),
        P("frame", "head"),
        P("frame", "head"),
        P(),
        P(),
        P("head", "frame"),
    )
    out_specs = P(("frame", "head"), None)
    return jax.shard_map(
        per_device, mesh=mesh, in_specs=in_specs, out_specs=out_specs, check_vma=False
    )
```

```python
import jax
import jax.numpy as jnp
from jax import lax
from jax.experimental import pallas as pl
from jax.experimental.pallas import tpu as pltpu
from jax.sharding import PartitionSpec as P

HD = 128
MESH = pl.DeviceIdType.MESH
F32 = jnp.float32
BF16 = jnp.bfloat16
NT = (((1,), (1,)), ((), ()))
NN = (((1,), (0,)), ((), ()))
SCALE = HD ** (-0.5)
DY = (0, 1, 2, 3, 6, 7, 4, 5)
GROUPS = ((0, 1), (1, 5), (6, 2))
FAR_FIRST = (4, 3, 5, 2, 6, 1, 7)


def dot(a, b, dims=NN):
    return lax.dot_general(a, b, dims, preferred_element_type=F32)


def send(src, dst, send_sem, recv_sem, **where):
    copy = pltpu.make_async_remote_copy(
        src_ref=src, dst_ref=dst, send_sem=send_sem, recv_sem=recv_sem,
        device_id=where, device_id_type=MESH,
    )
    copy.start()


def wait_for(ref, sem):
    pltpu.make_async_copy(ref, ref, sem).wait()


def one_hot(rows, cols, want):
    out = lax.broadcasted_iota(jnp.int32, (rows, cols), 0)
    src = lax.broadcasted_iota(jnp.int32, (rows, cols), 1)
    return jnp.where(src == want(out), 1.0, 0.0).astype(BF16)


def kernel(
    q_hbm, k_hbm, v_hbm, tk_hbm, tv_hbm, w_hbm, kinds_ref, count_ref, out_ref,
    qb, kb, vb, tkb, tvb, pack, got, turned, done, back, backed, wg, text32, text, toks, spat, mixed,
    part, rsend, rrecv,
    in_sem, f_s, f_r, b_s, b_r, ty_s, ty_r, tx_s, tx_r, tp_s, tp_r,
    wy_s, wy_r, wz_s, wz_r, wx_s, wx_r, wf_s, wf_r, wp_s, wp_r, rs_s, rs_r,
):
    frame = lax.axis_index("frame")
    z = lax.axis_index("head")
    y = frame // 8
    j = frame % 8
    x = j // 2
    core = j % 2

    def at(yy, jj):
        return yy * 8 + jj

    def turn(base, step, size):
        return (base + step + size) % size

    j_right = turn(x, 1, 4) * 2 + core
    j_left = turn(x, -1, 4) * 2 + core
    j_far = turn(x, 2, 4) * 2 + core
    shift = 1 - 2 * core
    partner = at(y, j + shift)

    barrier = pltpu.get_barrier_semaphore()

    def greet(i, carry):
        pl.semaphore_signal(barrier, inc=1, device_id={"frame": (frame + i) % 64}, device_id_type=MESH)
        return carry

    lax.fori_loop(1, 64, greet, 0)
    for k in (1, -1):
        pl.semaphore_signal(barrier, inc=1, device_id={"head": turn(z, k, 8)}, device_id_type=MESH)

    loads = [
        pltpu.make_async_copy(src, dst, in_sem.at[i])
        for i, (src, dst) in enumerate(
            ((q_hbm, qb), (k_hbm, kb), (v_hbm, vb), (tk_hbm, tkb), (tv_hbm, tvb), (w_hbm, wg.at[0, j]))
        )
    ]
    for load in loads:
        load.start()
    text32[...] = jnp.zeros_like(text32)
    loads[3].wait()
    loads[4].wait()
    for h in range(3):
        lanes = pl.ds(h * HD, HD)
        text32[h * 4:h * 4 + 4, :] = tkb[:, lanes].astype(F32)
        text32[12 + h * 4:16 + h * 4, :] = tvb[:, lanes].astype(F32)
    text[0, j] = text32[...].astype(BF16)
    for i, (load, buf) in enumerate(zip(loads, (qb, kb, vb))):
        load.wait()
        for h in range(3):
            units = buf[:, h * HD:(h + 1) * HD].reshape(8, 2, 16, HD)
            for half in range(2):
                pack[half, :, h, i * 16:(i + 1) * 16, :] = units[:, half]

    loads[5].wait()

    def unit_j(half, k):
        return 2 * k if half == 0 else (2 * k + 4) % 8 + 1

    active = [(j % 2) == 0, (j % 2) == 1]
    active = [
        jnp.logical_or(jnp.logical_or(j == unit_j(half, 0), j == unit_j(half, 1)), j == unit_j(half, 2))
        for half in range(2)
    ]
    my_k = [j // 2, ((j + 3) % 8) // 2]

    pl.semaphore_wait(barrier, 65)

    def text_y():
        for d in FAR_FIRST:
            send(text.at[0, j], text.at[d, j], ty_s.at[d], ty_r.at[d], frame=at(turn(y, -d, 8), j))

    def text_x():
        for d in range(1, 8):
            wait_for(text.at[d, j], ty_r.at[d])
        col = text.at[pl.ds(0, 8), j]
        for i, jj in enumerate((j_far, j_right, j_left)):
            send(col, col, tx_s.at[i], tx_r.at[i], frame=at(y, jj))
        send(col, col, tp_s.at[3], tp_r.at[3], frame=partner)

    def text_p():
        for i, jj in enumerate((j_far, j_left, j_right)):
            col = text.at[pl.ds(0, 8), jj]
            wait_for(col, tx_r.at[i])
            send(col, col, tp_s.at[i], tp_r.at[i], frame=partner)

    def text_done():
        for i, jj in enumerate((j_far, j_left, j_right, j)):
            wait_for(text.at[pl.ds(0, 8), jj + shift], tp_r.at[i])

    def forward(half):
        def one(i, carry):
            yy = (y + i) % 8
            for k in range(3):
                jj = unit_j(half, k)

                @pl.when(at(yy, jj) != frame)
                def _():
                    send(pack.at[half, yy, k], got.at[frame], f_s.at[half], f_r, frame=at(yy, jj))

            return carry

        lax.fori_loop(1, 9, one, 0)

        @pl.when(active[half])
        def _():
            got[frame] = pack[half, y, my_k[half]]

    def counted(half, ref, sem):
        @pl.when(active[half])
        def _():
            wait_for(ref.at[pl.ds(0, 23)], sem)

        @pl.when(jnp.logical_not(active[half]))
        def _():
            wait_for(ref.at[pl.ds(0, 24)], sem)

    def forward_sent(half):
        counted(half, got, f_s.at[half])

    def temporal(half):
        @pl.when(active[half])
        def _():
            wait_for(got.at[pl.ds(0, 63)], f_r)
            swap = one_hot(256, 256, lambda out: (out % 16) * 16 + out // 16)
            for c in range(4):
                rows = jnp.concatenate(
                    [got[c * 16:(c + 1) * 16, i * 16:(i + 1) * 16, :].reshape(256, HD) for i in range(3)],
                    axis=1,
                )
                rows = dot(swap, rows).astype(BF16)
                for i in range(3):
                    turned[i, :, c * 16:(c + 1) * 16, :] = rows[:, i * HD:(i + 1) * HD].reshape(16, 16, HD)
            row = lax.broadcasted_iota(jnp.int32, (256, 256), 0)
            col = lax.broadcasted_iota(jnp.int32, (256, 256), 1)
            same = (row // 64) == (col // 64)
            for g in range(4):
                qg, kg, vg = [turned[i, g * 4:(g + 1) * 4].reshape(256, HD) for i in range(3)]
                scores = jnp.where(same, dot(qg, kg, NT) * SCALE, -1e30)
                expo = jnp.exp(scores - jnp.max(scores, axis=1, keepdims=True))
                total = jnp.sum(expo, axis=1, keepdims=True)
                result = dot(expo.astype(BF16), vg) / total
                done[g * 4:(g + 1) * 4] = result.astype(BF16).reshape(4, 64, HD)
            for c in range(4):
                rows = dot(swap, done[:, c * 16:(c + 1) * 16, :].reshape(256, HD))
                back[c * 16:(c + 1) * 16] = rows.astype(BF16).reshape(16, 16, HD)

            def one(i, carry):
                to = (frame + i) % 64
                send(back.at[to], backed.at[half, y * 3 + my_k[half]], b_s, b_r.at[half], frame=to)
                return carry

            lax.fori_loop(1, 64, one, 0)
            backed[half, y * 3 + my_k[half]] = back[frame]

    def w_y1():
        for i, d in ((3, 3), (2, 2), (1, 1), (4, 6), (5, 7)):
            send(wg.at[0, j], wg.at[i, j], wy_s.at[i], wy_r.at[i], frame=at(turn(y, -d, 8), j))

    def w_y2():
        for i in range(1, 6):
            wait_for(wg.at[i, j], wy_r.at[i])
        for i, d in ((7, 2), (6, 1)):
            send(wg.at[3, j], wg.at[i, j], wz_s.at[i - 6], wz_r.at[i - 6], frame=at(turn(y, -d, 8), j))

    def w_y3():
        for i in (6, 7):
            wait_for(wg.at[i, j], wz_r.at[i - 6])

    def cut(group, jj):
        first, count = GROUPS[group]
        return wg.at[pl.ds(first, count), jj]

    def w_x1(group):
        src = cut(group, j)
        send(src, src, wx_s.at[0, group], wx_r.at[0, group], frame=at(y, j_right))
        send(src, src, wx_s.at[1, group], wx_r.at[1, group], frame=at(y, j_left))
        send(src, src, wp_s.at[0, group], wp_r.at[0, group], frame=partner)

    def w_x2(group):
        src = cut(group, j_right)
        wait_for(src, wx_r.at[1, group])
        send(src, src, wf_s.at[group], wf_r.at[group], frame=at(y, j_left))
        send(src, src, wp_s.at[1, group], wp_r.at[1, group], frame=partner)
        src = cut(group, j_left)
        wait_for(src, wx_r.at[0, group])
        send(src, src, wp_s.at[2, group], wp_r.at[2, group], frame=partner)

    def w_x3(group):
        src = cut(group, j_far)
        wait_for(src, wf_r.at[group])
        send(src, src, wp_s.at[3, group], wp_r.at[3, group], frame=partner)

    def w_done(group):
        for i, jj in enumerate((j, j_right, j_left, j_far)):
            wait_for(cut(group, jj + shift), wp_r.at[i, group])

    def spatial():
        pick = one_hot(192, 256, lambda out: ((out % 32) // 4) * 32 + (out // 32) * 4 + out % 4)
        for d in range(8):
            rows = dot(pick, text[d].reshape(256, HD)).astype(BF16)
            toks[:, d * 32:(d + 1) * 32, :] = rows.reshape(6, 32, HD)
        col = lax.broadcasted_iota(jnp.int32, (256, 256), 1)
        live = (y * 32 + col) % 256 < count_ref[0]
        for h in range(3):
            lanes = pl.ds(h * HD, HD)
            qh = qb[:, lanes]
            own = dot(qh, kb[:, lanes], NT) * SCALE
            other = jnp.where(live, dot(qh, toks[h], NT) * SCALE, -1e30)
            top = jnp.maximum(
                jnp.max(own, axis=1, keepdims=True), jnp.max(other, axis=1, keepdims=True)
            )
            e_own = jnp.exp(own - top)
            e_other = jnp.exp(other - top)
            total = jnp.sum(e_own, axis=1, keepdims=True) + jnp.sum(e_other, axis=1, keepdims=True)
            result = dot(e_own.astype(BF16), vb[:, lanes]) + dot(e_other.astype(BF16), toks[3 + h])
            spat[:, :, :, lanes] = (result / total).astype(BF16).reshape(8, 2, 16, HD)

    def length(pair, way):
        return 4 if (pair + way) % 2 == 0 else 3

    def dest(pair, way, stage):
        left = length(pair, way) - stage
        return turn(z, left if way == 0 else -left, 8)

    def pass_on(src, half, pair, way, stage):
        at_sem = (half, way, pair, stage)
        send(src, rrecv.at[at_sem], rs_s.at[at_sem], rs_r.at[at_sem], head=turn(z, 1 - 2 * way, 8))

    def mix(half):
        counted(half, backed.at[half], b_r.at[half])
        for h in range(3):
            lanes = pl.ds(h * HD, HD)
            temp = backed[half].reshape(8, 3, 16, HD)[:, h].reshape(128, HD)
            own = spat[:, half, :, lanes].reshape(128, HD)
            mixed[half, :, lanes] = jnp.where(kinds_ref[z * 3 + h] == 1, temp, own)

    def project(half, pair):
        for i in range(2):
            term = dot(mixed[half], wg[pair * 2 + i].reshape(384, 384), NT)
            part[half, pair, :, i] = term.astype(BF16).reshape(8, 16, 384)
        for way in range(2):
            pass_on(part.at[half, pair, dest(pair, way, 0)], half, pair, way, 0)

    def reduce(half, stage):
        for pair in range(4):
            for way in range(2):
                if stage < length(pair, way):
                    before = (half, way, pair, stage - 1)
                    now = (half, way, pair, stage)
                    wait_for(rrecv.at[before], rs_r.at[before])
                    own = part[half, pair, dest(pair, way, stage)].astype(F32)
                    rsend[now] = (own + rrecv[before].astype(F32)).astype(BF16)
                    pass_on(rsend.at[now], half, pair, way, stage)

    def finish(half):
        for pair in range(4):
            own = part[half, pair, z].astype(F32)
            for way in range(2):
                last = (half, way, pair, length(pair, way) - 1)
                wait_for(rrecv.at[last], rs_r.at[last])
                own = own + rrecv[last].astype(F32)
            for i in range(2):
                block = turn(y, DY[pair * 2 + i], 8)
                columns = pl.ds(pl.multiple_of(block * 384, 384), 384)
                out_ref[half * 16:(half + 1) * 16, columns] = own[i].astype(BF16)

    def drain_rs(half):
        for pair in range(4):
            for way in range(2):
                for stage in range(length(pair, way)):
                    now = (half, way, pair, stage)
                    wait_for(rrecv.at[now], rs_s.at[now])

    def drain_text():
        for d in range(1, 8):
            wait_for(text.at[d, j], ty_s.at[d])
        col = text.at[pl.ds(0, 8), j]
        for i in range(3):
            wait_for(col, tx_s.at[i])
        for i in range(4):
            wait_for(col, tp_s.at[i])

    def drain_w():
        for i in range(1, 6):
            wait_for(wg.at[i, j], wy_s.at[i])
        for i in range(2):
            wait_for(wg.at[i, j], wz_s.at[i])
        for group in range(3):
            wait_for(cut(group, j), wx_s.at[0, group])
            wait_for(cut(group, j), wx_s.at[1, group])
            wait_for(cut(group, j), wf_s.at[group])
            for i in range(4):
                wait_for(cut(group, j), wp_s.at[i, group])

    def drain_back():
        @pl.when(jnp.logical_or(active[0], active[1]))
        def _():
            wait_for(back.at[pl.ds(0, 63)], b_s)

    w_y1()
    w_x1(0)
    text_y()
    forward(0)
    w_y2()
    w_x1(1)
    w_x2(0)
    text_x()
    forward_sent(0)
    forward(1)
    w_y3()
    w_x1(2)
    w_x2(1)
    w_x3(0)
    temporal(0)
    text_p()
    text_done()
    spatial()
    w_x2(2)
    w_x3(1)
    w_x3(2)
    w_done(0)
    w_done(1)
    w_done(2)
    mix(0)
    project(0, 0)
    project(0, 1)
    project(0, 2)
    project(0, 3)
    temporal(1)
    reduce(0, 1)
    reduce(0, 2)
    mix(1)
    project(1, 0)
    project(1, 1)
    project(1, 2)
    project(1, 3)
    reduce(0, 3)
    reduce(1, 1)
    reduce(1, 2)
    reduce(1, 3)
    finish(0)
    finish(1)
    forward_sent(1)
    drain_rs(0)
    drain_rs(1)
    drain_text()
    drain_w()
    drain_back()


def per_device(queries, keys, values, text_keys, text_values, head_kinds, text_count, w_out):
    anywhere = pl.BlockSpec(memory_space=pl.ANY)
    vmem = pl.BlockSpec(memory_space=pltpu.VMEM)
    smem = pl.BlockSpec(memory_space=pltpu.SMEM)
    dma = pltpu.SemaphoreType.DMA
    return pl.pallas_call(
        kernel,
        out_shape=jax.ShapeDtypeStruct((32, 3072), BF16),
        in_specs=[anywhere] * 6 + [smem] * 2,
        out_specs=vmem,
        scratch_shapes=[
            pltpu.VMEM((256, 384), BF16),
            pltpu.VMEM((256, 384), BF16),
            pltpu.VMEM((256, 384), BF16),
            pltpu.VMEM((4, 384), BF16),
            pltpu.VMEM((4, 384), BF16),
            pltpu.VMEM((2, 8, 3, 48, HD), BF16),
            pltpu.VMEM((64, 48, HD), BF16),
            pltpu.VMEM((3, 16, 64, HD), BF16),
            pltpu.VMEM((16, 64, HD), BF16),
            pltpu.VMEM((64, 16, HD), BF16),
            pltpu.VMEM((2, 24, 16, HD), BF16),
            pltpu.VMEM((8, 8, 48, 384), BF16),
            pltpu.VMEM((32, HD), F32),
            pltpu.VMEM((8, 8, 32, HD), BF16),
            pltpu.VMEM((6, 256, HD), BF16),
            pltpu.VMEM((8, 2, 16, 384), BF16),
            pltpu.VMEM((2, 128, 384), BF16),
            pltpu.VMEM((2, 4, 8, 2, 16, 384), BF16),
            pltpu.VMEM((2, 2, 4, 4, 2, 16, 384), BF16),
            pltpu.VMEM((2, 2, 4, 4, 2, 16, 384), BF16),
            dma((6,)),
            dma((2,)),
            dma,
            dma,
            dma((2,)),
            dma((8,)),
            dma((8,)),
            dma((3,)),
            dma((3,)),
            dma((4,)),
            dma((4,)),
            dma((6,)),
            dma((6,)),
            dma((2,)),
            dma((2,)),
            dma((2, 3)),
            dma((2, 3)),
            dma((3,)),
            dma((3,)),
            dma((4, 3)),
            dma((4, 3)),
            dma((2, 2, 4, 4)),
            dma((2, 2, 4, 4)),
        ],
        compiler_params=pltpu.CompilerParams(
            collective_id=0, has_side_effects=True, vmem_limit_bytes=60 * 1024 * 1024
        ),
    )(queries, keys, values, text_keys, text_values, w_out.T, head_kinds, text_count)


def solution(mesh):
    in_specs = (
        P("frame", "head"),
        P("frame", "head"),
        P("frame", "head"),
        P("frame", "head"),
        P("frame", "head"),
        P(),
        P(),
        P("head", "frame"),
    )
    out_specs = P(("frame", "head"), None)
    return jax.shard_map(
        per_device, mesh=mesh, in_specs=in_specs, out_specs=out_specs, check_vma=False
    )
```

```python
import jax
import jax.numpy as jnp
from jax import lax
from jax.experimental import pallas as pl
from jax.experimental.pallas import tpu as pltpu
from jax.sharding import PartitionSpec as P

HD = 128
MESH = pl.DeviceIdType.MESH
F32 = jnp.float32
BF16 = jnp.bfloat16
NT = (((1,), (1,)), ((), ()))
NN = (((1,), (0,)), ((), ()))
SCALE = HD ** (-0.5)
DY = (0, 1, 7, 2, 6, 3, 4, 5)
BATCHES = ((4, 7), (3, 6), (2, 5), (1, 0))
GROUPS = ((0, 1), (1, 2), (3, 2), (5, 1), (6, 2))
ONWARD = (1, 0, 1, 0, 1)
FAR_FIRST = (4, 3, 5, 2, 6, 1, 7)


def dot(a, b, dims=NN):
    return lax.dot_general(a, b, dims, preferred_element_type=F32)


def send(src, dst, send_sem, recv_sem, **where):
    copy = pltpu.make_async_remote_copy(
        src_ref=src, dst_ref=dst, send_sem=send_sem, recv_sem=recv_sem,
        device_id=where, device_id_type=MESH,
    )
    copy.start()


def wait_for(ref, sem):
    pltpu.make_async_copy(ref, ref, sem).wait()


def one_hot(rows, cols, want):
    out = lax.broadcasted_iota(jnp.int32, (rows, cols), 0)
    src = lax.broadcasted_iota(jnp.int32, (rows, cols), 1)
    return jnp.where(src == want(out), 1.0, 0.0).astype(BF16)


def kernel(
    q_hbm, k_hbm, v_hbm, tk_hbm, tv_hbm, w_hbm, kinds_ref, count_ref, out_ref,
    qb, kb, vb, tkb, tvb, pack, got, turned, done, back, backed, wg, text32, text, toks, spat, mixed,
    part, rsend, rrecv,
    in_sem, f_s, f_r, b_s, b_r, ty_s, ty_r, tx_s, tx_r, tp_s, tp_r,
    wy_s, wy_r, wx_s, wx_r, wf_s, wf_r, wp_s, wp_r, rs_s, rs_r,
):
    frame = lax.axis_index("frame")
    z = lax.axis_index("head")
    y = frame // 8
    j = frame % 8
    x = j // 2
    core = j % 2

    def at(yy, jj):
        return yy * 8 + jj

    def turn(base, step, size):
        return (base + step + size) % size

    j_right = turn(x, 1, 4) * 2 + core
    j_left = turn(x, -1, 4) * 2 + core
    j_far = turn(x, 2, 4) * 2 + core
    shift = 1 - 2 * core
    partner = at(y, j + shift)

    barrier = pltpu.get_barrier_semaphore()

    def greet(i, carry):
        pl.semaphore_signal(barrier, inc=1, device_id={"frame": (frame + i) % 64}, device_id_type=MESH)
        return carry

    lax.fori_loop(1, 64, greet, 0)
    for k in (1, -1):
        pl.semaphore_signal(barrier, inc=1, device_id={"head": turn(z, k, 8)}, device_id_type=MESH)

    loads = [
        pltpu.make_async_copy(src, dst, in_sem.at[i])
        for i, (src, dst) in enumerate(
            ((q_hbm, qb), (k_hbm, kb), (v_hbm, vb), (tk_hbm, tkb), (tv_hbm, tvb), (w_hbm, wg.at[0, j]))
        )
    ]
    for load in loads:
        load.start()
    text32[...] = jnp.zeros_like(text32)
    loads[3].wait()
    loads[4].wait()
    for h in range(3):
        lanes = pl.ds(h * HD, HD)
        text32[h * 4:h * 4 + 4, :] = tkb[:, lanes].astype(F32)
        text32[12 + h * 4:16 + h * 4, :] = tvb[:, lanes].astype(F32)
    text[0, j] = text32[...].astype(BF16)
    for i, (load, buf) in enumerate(zip(loads, (qb, kb, vb))):
        load.wait()
        for h in range(3):
            units = buf[:, h * HD:(h + 1) * HD].reshape(8, 2, 16, HD)
            for half in range(2):
                pack[half, :, h, i * 16:(i + 1) * 16, :] = units[:, half]

    loads[5].wait()

    def unit_j(half, yy, k):
        return ((yy + k) % 4) * 2 + half

    my_k = (x - y + 8) % 4
    active = [jnp.logical_and(core == half, my_k < 3) for half in range(2)]

    pl.semaphore_wait(barrier, 65)

    def text_y():
        for d in FAR_FIRST:
            send(text.at[0, j], text.at[d, j], ty_s.at[d], ty_r.at[d], frame=at(turn(y, -d, 8), j))

    def text_x():
        for d in range(1, 8):
            wait_for(text.at[d, j], ty_r.at[d])
        col = text.at[pl.ds(0, 8), j]
        send(col, col, tx_s.at[0], tx_r.at[0], frame=at(y, j_left))
        send(col, col, tx_s.at[1], tx_r.at[1], frame=at(y, j_right))
        send(col, col, tp_s.at[3], tp_r.at[3], frame=partner)

    def text_x2():
        col = text.at[pl.ds(0, 8), j_right]
        wait_for(col, tx_r.at[0])
        send(col, col, tx_s.at[2], tx_r.at[2], frame=at(y, j_left))
        send(col, col, tp_s.at[2], tp_r.at[2], frame=partner)
        col = text.at[pl.ds(0, 8), j_left]
        wait_for(col, tx_r.at[1])
        send(col, col, tp_s.at[1], tp_r.at[1], frame=partner)

    def text_p():
        col = text.at[pl.ds(0, 8), j_far]
        wait_for(col, tx_r.at[2])
        send(col, col, tp_s.at[0], tp_r.at[0], frame=partner)

    def text_done():
        for i, jj in enumerate((j_far, j_left, j_right, j)):
            wait_for(text.at[pl.ds(0, 8), jj + shift], tp_r.at[i])

    def forward(half, batch):
        for d in BATCHES[batch]:
            yy = turn(y, d, 8)
            for k in range(3):
                jj = unit_j(half, yy, k)

                def one():
                    send(pack.at[half, yy, k], got.at[frame], f_s.at[half, batch], f_r, frame=at(yy, jj))

                if d == 0:
                    pl.when(j != jj)(one)
                else:
                    one()
        if 0 in BATCHES[batch]:
            @pl.when(active[half])
            def _():
                got[frame] = pack[half, y, my_k]

    def counted(half, ref, count, sem):
        @pl.when(active[half])
        def _():
            wait_for(ref.at[pl.ds(0, count - 1)], sem)

        @pl.when(jnp.logical_not(active[half]))
        def _():
            wait_for(ref.at[pl.ds(0, count)], sem)

    def forward_sent(half, batch):
        if 0 in BATCHES[batch]:
            counted(half, got, 6, f_s.at[half, batch])
        else:
            wait_for(got.at[pl.ds(0, 6)], f_s.at[half, batch])

    def temporal(half):
        @pl.when(active[half])
        def _():
            wait_for(got.at[pl.ds(0, 63)], f_r)
            swap = one_hot(256, 256, lambda out: (out % 16) * 16 + out // 16)
            for c in range(4):
                rows = jnp.concatenate(
                    [got[c * 16:(c + 1) * 16, i * 16:(i + 1) * 16, :].reshape(256, HD) for i in range(3)],
                    axis=1,
                )
                rows = dot(swap, rows).astype(BF16)
                for i in range(3):
                    turned[i, :, c * 16:(c + 1) * 16, :] = rows[:, i * HD:(i + 1) * HD].reshape(16, 16, HD)
            row = lax.broadcasted_iota(jnp.int32, (256, 256), 0)
            col = lax.broadcasted_iota(jnp.int32, (256, 256), 1)
            same = (row // 64) == (col // 64)
            for g in range(4):
                qg, kg, vg = [turned[i, g * 4:(g + 1) * 4].reshape(256, HD) for i in range(3)]
                scores = jnp.where(same, dot(qg, kg, NT) * SCALE, -1e30)
                expo = jnp.exp(scores - jnp.max(scores, axis=1, keepdims=True))
                total = jnp.sum(expo, axis=1, keepdims=True)
                result = dot(expo.astype(BF16), vg) / total
                done[g * 4:(g + 1) * 4] = result.astype(BF16).reshape(4, 64, HD)
            for c in range(4):
                rows = dot(swap, done[:, c * 16:(c + 1) * 16, :].reshape(256, HD))
                back[c * 16:(c + 1) * 16] = rows.astype(BF16).reshape(16, 16, HD)

            def one(i, carry):
                to = (frame + i) % 64
                send(back.at[to], backed.at[half, y * 3 + my_k], b_s, b_r.at[half], frame=to)
                return carry

            lax.fori_loop(1, 64, one, 0)
            backed[half, y * 3 + my_k] = back[frame]

    def w_y1():
        for i in range(1, 6):
            send(wg.at[0, j], wg.at[i, j], wy_s.at[i], wy_r.at[i], frame=at(turn(y, -DY[i], 8), j))

    def w_y2(group):
        first, count = GROUPS[group]
        for i in range(first, first + count):
            wait_for(wg.at[i, j], wy_r.at[i])
            if i in (4, 5):
                to, way = (7, 1) if i == 4 else (6, -1)
                send(wg.at[i, j], wg.at[to, j], wy_s.at[to], wy_r.at[to], frame=at(turn(y, way, 8), j))

    def cut(group, jj):
        first, count = GROUPS[group]
        return wg.at[pl.ds(first, count), jj]

    def w_x1(group):
        src = cut(group, j)
        send(src, src, wx_s.at[0, group], wx_r.at[0, group], frame=at(y, j_right))
        send(src, src, wx_s.at[1, group], wx_r.at[1, group], frame=at(y, j_left))
        send(src, src, wp_s.at[0, group], wp_r.at[0, group], frame=partner)

    def w_x2(group):
        for way, jj in ((1, j_right), (0, j_left)):
            src = cut(group, jj)
            wait_for(src, wx_r.at[way, group])
            if way == ONWARD[group]:
                to = j_left if way == 1 else j_right
                send(src, src, wf_s.at[group], wf_r.at[group], frame=at(y, to))
            send(src, src, wp_s.at[2 - way, group], wp_r.at[2 - way, group], frame=partner)

    def w_x3(group):
        src = cut(group, j_far)
        wait_for(src, wf_r.at[group])
        send(src, src, wp_s.at[3, group], wp_r.at[3, group], frame=partner)

    def w_done(group):
        for i, jj in enumerate((j, j_right, j_left, j_far)):
            wait_for(cut(group, jj + shift), wp_r.at[i, group])

    def spatial():
        pick = one_hot(192, 256, lambda out: ((out % 32) // 4) * 32 + (out // 32) * 4 + out % 4)
        for d in range(8):
            rows = dot(pick, text[d].reshape(256, HD)).astype(BF16)
            toks[:, d * 32:(d + 1) * 32, :] = rows.reshape(6, 32, HD)
        col = lax.broadcasted_iota(jnp.int32, (256, 256), 1)
        live = (y * 32 + col) % 256 < count_ref[0]
        for h in range(3):
            lanes = pl.ds(h * HD, HD)
            qh = qb[:, lanes]
            own = dot(qh, kb[:, lanes], NT) * SCALE
            other = jnp.where(live, dot(qh, toks[h], NT) * SCALE, -1e30)
            top = jnp.maximum(
                jnp.max(own, axis=1, keepdims=True), jnp.max(other, axis=1, keepdims=True)
            )
            e_own = jnp.exp(own - top)
            e_other = jnp.exp(other - top)
            total = jnp.sum(e_own, axis=1, keepdims=True) + jnp.sum(e_other, axis=1, keepdims=True)
            result = dot(e_own.astype(BF16), vb[:, lanes]) + dot(e_other.astype(BF16), toks[3 + h])
            spat[:, :, :, lanes] = (result / total).astype(BF16).reshape(8, 2, 16, HD)

    def length(pair, way):
        return 4 if (pair + way) % 2 == 0 else 3

    def dest(pair, way, stage):
        left = length(pair, way) - stage
        return turn(z, left if way == 0 else -left, 8)

    def pass_on(src, half, pair, way, stage):
        at_sem = (half, way, pair, stage)
        send(src, rrecv.at[at_sem], rs_s.at[at_sem], rs_r.at[at_sem], head=turn(z, 1 - 2 * way, 8))

    def mix(half):
        counted(half, backed.at[half], 24, b_r.at[half])
        for h in range(3):
            lanes = pl.ds(h * HD, HD)
            temp = backed[half].reshape(8, 3, 16, HD)[:, h].reshape(128, HD)
            own = spat[:, half, :, lanes].reshape(128, HD)
            mixed[half, :, lanes] = jnp.where(kinds_ref[z * 3 + h] == 1, temp, own)

    def project(half, pair):
        for i in range(2):
            term = dot(mixed[half], wg[pair * 2 + i].reshape(384, 384), NT)
            part[half, pair, :, i] = term.astype(BF16).reshape(8, 16, 384)
        for way in range(2):
            pass_on(part.at[half, pair, dest(pair, way, 0)], half, pair, way, 0)

    def reduce(half, stage):
        for pair in range(4):
            for way in range(2):
                if stage < length(pair, way):
                    before = (half, way, pair, stage - 1)
                    now = (half, way, pair, stage)
                    wait_for(rrecv.at[before], rs_r.at[before])
                    own = part[half, pair, dest(pair, way, stage)].astype(F32)
                    rsend[now] = (own + rrecv[before].astype(F32)).astype(BF16)
                    pass_on(rsend.at[now], half, pair, way, stage)

    def finish(half):
        for pair in range(4):
            own = part[half, pair, z].astype(F32)
            for way in range(2):
                last = (half, way, pair, length(pair, way) - 1)
                wait_for(rrecv.at[last], rs_r.at[last])
                own = own + rrecv[last].astype(F32)
            for i in range(2):
                block = turn(y, DY[pair * 2 + i], 8)
                columns = pl.ds(pl.multiple_of(block * 384, 384), 384)
                out_ref[half * 16:(half + 1) * 16, columns] = own[i].astype(BF16)

    def drain_rs(half):
        for pair in range(4):
            for way in range(2):
                for stage in range(length(pair, way)):
                    now = (half, way, pair, stage)
                    wait_for(rrecv.at[now], rs_s.at[now])

    def drain_text():
        for d in range(1, 8):
            wait_for(text.at[d, j], ty_s.at[d])
        col = text.at[pl.ds(0, 8), j]
        for i in range(3):
            wait_for(col, tx_s.at[i])
        for i in range(4):
            wait_for(col, tp_s.at[i])

    def drain_w():
        for i in range(1, 8):
            wait_for(wg.at[i, j], wy_s.at[i])
        for group in range(5):
            wait_for(cut(group, j), wx_s.at[0, group])
            wait_for(cut(group, j), wx_s.at[1, group])
            wait_for(cut(group, j), wf_s.at[group])
            for i in range(4):
                wait_for(cut(group, j), wp_s.at[i, group])

    def drain_back():
        @pl.when(jnp.logical_or(active[0], active[1]))
        def _():
            wait_for(back.at[pl.ds(0, 63)], b_s)

    w_y1()
    w_x1(0)
    text_y()
    forward(0, 0)
    forward(0, 1)
    forward(0, 2)
    forward(0, 3)
    w_y2(1)
    w_x1(1)
    w_y2(2)
    w_x1(2)
    w_x2(0)
    w_y2(3)
    w_x1(3)
    text_x()
    forward(1, 0)
    forward(1, 1)
    forward(1, 2)
    forward(1, 3)
    temporal(0)
    w_x2(1)
    w_x2(2)
    w_y2(4)
    w_x1(4)
    w_x3(0)
    text_x2()
    w_x2(3)
    w_x3(1)
    w_x3(2)
    w_x2(4)
    temporal(1)
    text_p()
    w_x3(3)
    text_done()
    spatial()
    w_done(0)
    w_done(1)
    mix(0)
    project(0, 0)
    w_x3(4)
    w_done(2)
    project(0, 1)
    w_done(3)
    project(0, 2)
    mix(1)
    project(1, 0)
    project(1, 1)
    project(1, 2)
    w_done(4)
    project(0, 3)
    project(1, 3)
    reduce(0, 1)
    reduce(1, 1)
    reduce(0, 2)
    reduce(1, 2)
    reduce(0, 3)
    reduce(1, 3)
    finish(0)
    finish(1)
    forward_sent(0, 0)
    forward_sent(0, 1)
    forward_sent(0, 2)
    forward_sent(0, 3)
    forward_sent(1, 0)
    forward_sent(1, 1)
    forward_sent(1, 2)
    forward_sent(1, 3)
    drain_rs(0)
    drain_rs(1)
    drain_text()
    drain_w()
    drain_back()


def per_device(queries, keys, values, text_keys, text_values, head_kinds, text_count, w_out):
    anywhere = pl.BlockSpec(memory_space=pl.ANY)
    vmem = pl.BlockSpec(memory_space=pltpu.VMEM)
    smem = pl.BlockSpec(memory_space=pltpu.SMEM)
    dma = pltpu.SemaphoreType.DMA
    return pl.pallas_call(
        kernel,
        out_shape=jax.ShapeDtypeStruct((32, 3072), BF16),
        in_specs=[anywhere] * 6 + [smem] * 2,
        out_specs=vmem,
        scratch_shapes=[
            pltpu.VMEM((256, 384), BF16),
            pltpu.VMEM((256, 384), BF16),
            pltpu.VMEM((256, 384), BF16),
            pltpu.VMEM((4, 384), BF16),
            pltpu.VMEM((4, 384), BF16),
            pltpu.VMEM((2, 8, 3, 48, HD), BF16),
            pltpu.VMEM((64, 48, HD), BF16),
            pltpu.VMEM((3, 16, 64, HD), BF16),
            pltpu.VMEM((16, 64, HD), BF16),
            pltpu.VMEM((64, 16, HD), BF16),
            pltpu.VMEM((2, 24, 16, HD), BF16),
            pltpu.VMEM((8, 8, 48, 384), BF16),
            pltpu.VMEM((32, HD), F32),
            pltpu.VMEM((8, 8, 32, HD), BF16),
            pltpu.VMEM((6, 256, HD), BF16),
            pltpu.VMEM((8, 2, 16, 384), BF16),
            pltpu.VMEM((2, 128, 384), BF16),
            pltpu.VMEM((2, 4, 8, 2, 16, 384), BF16),
            pltpu.VMEM((2, 2, 4, 4, 2, 16, 384), BF16),
            pltpu.VMEM((2, 2, 4, 4, 2, 16, 384), BF16),
            dma((6,)),
            dma((2, 4)),
            dma,
            dma,
            dma((2,)),
            dma((8,)),
            dma((8,)),
            dma((3,)),
            dma((3,)),
            dma((4,)),
            dma((4,)),
            dma((8,)),
            dma((8,)),
            dma((2, 5)),
            dma((2, 5)),
            dma((5,)),
            dma((5,)),
            dma((4, 5)),
            dma((4, 5)),
            dma((2, 2, 4, 4)),
            dma((2, 2, 4, 4)),
        ],
        compiler_params=pltpu.CompilerParams(
            collective_id=0, has_side_effects=True, vmem_limit_bytes=60 * 1024 * 1024
        ),
    )(queries, keys, values, text_keys, text_values, w_out.T, head_kinds, text_count)


def solution(mesh):
    in_specs = (
        P("frame", "head"),
        P("frame", "head"),
        P("frame", "head"),
        P("frame", "head"),
        P("frame", "head"),
        P(),
        P(),
        P("head", "frame"),
    )
    out_specs = P(("frame", "head"), None)
    return jax.shard_map(
        per_device, mesh=mesh, in_specs=in_specs, out_specs=out_specs, check_vma=False
    )
```

```python
import jax
import jax.numpy as jnp
from jax import lax
from jax.experimental import pallas as pl
from jax.experimental.pallas import tpu as pltpu
from jax.sharding import PartitionSpec as P

HD = 128
MESH = pl.DeviceIdType.MESH
F32 = jnp.float32
BF16 = jnp.bfloat16
NT = (((1,), (1,)), ((), ()))
NN = (((1,), (0,)), ((), ()))
SCALE = HD ** (-0.5)
DY = (0, 1, 7, 2, 6, 3, 4, 5)
BATCHES = ((4, 7), (3, 6), (2, 5), (1, 0))
GROUPS = ((0, 1), (1, 2), (3, 2), (5, 1), (6, 2))
ONWARD = (1, 0, 1, 0, 1)
FAR_FIRST = (4, 3, 5, 2, 6, 1, 7)


def dot(a, b, dims=NN):
    return lax.dot_general(a, b, dims, preferred_element_type=F32)


def send(src, dst, send_sem, recv_sem, **where):
    copy = pltpu.make_async_remote_copy(
        src_ref=src, dst_ref=dst, send_sem=send_sem, recv_sem=recv_sem,
        device_id=where, device_id_type=MESH,
    )
    copy.start()


def wait_for(ref, sem):
    pltpu.make_async_copy(ref, ref, sem).wait()


def one_hot(rows, cols, want):
    out = lax.broadcasted_iota(jnp.int32, (rows, cols), 0)
    src = lax.broadcasted_iota(jnp.int32, (rows, cols), 1)
    return jnp.where(src == want(out), 1.0, 0.0).astype(BF16)


def kernel(
    q_hbm, k_hbm, v_hbm, tk_hbm, tv_hbm, w_hbm, kinds_ref, count_ref, out_ref,
    qb, kb, vb, tkb, tvb, pack, got, turned, done, back, backed, wg, text32, text, toks, spat, mixed,
    part, rsend, rrecv,
    in_sem, f_s, f_r, b_s, b_r, ty_s, ty_r, tx_s, tx_r, tp_s, tp_r,
    wy_s, wy_r, wx_s, wx_r, wf_s, wf_r, wp_s, wp_r, rs_s, rs_r,
):
    frame = lax.axis_index("frame")
    z = lax.axis_index("head")
    y = frame // 8
    j = frame % 8
    x = j // 2
    core = j % 2

    def at(yy, jj):
        return yy * 8 + jj

    def turn(base, step, size):
        return (base + step + size) % size

    j_right = turn(x, 1, 4) * 2 + core
    j_left = turn(x, -1, 4) * 2 + core
    j_far = turn(x, 2, 4) * 2 + core
    shift = 1 - 2 * core
    partner = at(y, j + shift)

    barrier = pltpu.get_barrier_semaphore()

    def greet(i, carry):
        pl.semaphore_signal(barrier, inc=1, device_id={"frame": (frame + i) % 64}, device_id_type=MESH)
        return carry

    lax.fori_loop(1, 64, greet, 0)
    for k in (1, -1):
        pl.semaphore_signal(barrier, inc=1, device_id={"head": turn(z, k, 8)}, device_id_type=MESH)

    loads = [
        pltpu.make_async_copy(src, dst, in_sem.at[i])
        for i, (src, dst) in enumerate(
            ((q_hbm, qb), (k_hbm, kb), (v_hbm, vb), (tk_hbm, tkb), (tv_hbm, tvb), (w_hbm, wg.at[0, j]))
        )
    ]
    for load in loads:
        load.start()
    text32[...] = jnp.zeros_like(text32)
    loads[3].wait()
    loads[4].wait()
    for h in range(3):
        lanes = pl.ds(h * HD, HD)
        text32[h * 4:h * 4 + 4, :] = tkb[:, lanes].astype(F32)
        text32[12 + h * 4:16 + h * 4, :] = tvb[:, lanes].astype(F32)
    text[0, j] = text32[...].astype(BF16)
    for i, (load, buf) in enumerate(zip(loads, (qb, kb, vb))):
        load.wait()
        for h in range(3):
            units = buf[:, h * HD:(h + 1) * HD].reshape(8, 2, 16, HD)
            for half in range(2):
                pack[half, :, h, i * 16:(i + 1) * 16, :] = units[:, half]

    loads[5].wait()

    def unit_j(half, yy, k):
        return ((yy + k) % 4) * 2 + half

    my_k = (x - y + 8) % 4
    active = [jnp.logical_and(core == half, my_k < 3) for half in range(2)]

    pl.semaphore_wait(barrier, 65)

    def text_y():
        for d in FAR_FIRST:
            send(text.at[0, j], text.at[d, j], ty_s.at[d], ty_r.at[d], frame=at(turn(y, -d, 8), j))

    def text_x():
        for d in range(1, 8):
            wait_for(text.at[d, j], ty_r.at[d])
        col = text.at[pl.ds(0, 8), j]
        send(col, col, tx_s.at[0], tx_r.at[0], frame=at(y, j_left))
        send(col, col, tx_s.at[1], tx_r.at[1], frame=at(y, j_right))
        send(col, col, tp_s.at[3], tp_r.at[3], frame=partner)

    def text_x2():
        col = text.at[pl.ds(0, 8), j_right]
        wait_for(col, tx_r.at[0])
        send(col, col, tx_s.at[2], tx_r.at[2], frame=at(y, j_left))
        send(col, col, tp_s.at[2], tp_r.at[2], frame=partner)
        col = text.at[pl.ds(0, 8), j_left]
        wait_for(col, tx_r.at[1])
        send(col, col, tp_s.at[1], tp_r.at[1], frame=partner)

    def text_p():
        col = text.at[pl.ds(0, 8), j_far]
        wait_for(col, tx_r.at[2])
        send(col, col, tp_s.at[0], tp_r.at[0], frame=partner)

    def text_done():
        for i, jj in enumerate((j_far, j_left, j_right, j)):
            wait_for(text.at[pl.ds(0, 8), jj + shift], tp_r.at[i])

    def forward(half, batch):
        for d in BATCHES[batch]:
            yy = turn(y, d, 8)
            for k in range(3):
                jj = unit_j(half, yy, k)

                def one():
                    send(pack.at[half, yy, k], got.at[frame], f_s.at[half, batch], f_r, frame=at(yy, jj))

                if d == 0:
                    pl.when(j != jj)(one)
                else:
                    one()
        if 0 in BATCHES[batch]:
            @pl.when(active[half])
            def _():
                got[frame] = pack[half, y, my_k]

    def counted(half, ref, count, sem):
        @pl.when(active[half])
        def _():
            wait_for(ref.at[pl.ds(0, count - 1)], sem)

        @pl.when(jnp.logical_not(active[half]))
        def _():
            wait_for(ref.at[pl.ds(0, count)], sem)

    def forward_sent(half, batch):
        if 0 in BATCHES[batch]:
            counted(half, got, 6, f_s.at[half, batch])
        else:
            wait_for(got.at[pl.ds(0, 6)], f_s.at[half, batch])

    def temporal(half):
        @pl.when(active[half])
        def _():
            wait_for(got.at[pl.ds(0, 63)], f_r)
            swap = one_hot(256, 256, lambda out: (out % 16) * 16 + out // 16)
            for c in range(4):
                rows = jnp.concatenate(
                    [got[c * 16:(c + 1) * 16, i * 16:(i + 1) * 16, :].reshape(256, HD) for i in range(3)],
                    axis=1,
                )
                rows = dot(swap, rows).astype(BF16)
                for i in range(3):
                    turned[i, :, c * 16:(c + 1) * 16, :] = rows[:, i * HD:(i + 1) * HD].reshape(16, 16, HD)
            row = lax.broadcasted_iota(jnp.int32, (256, 256), 0)
            col = lax.broadcasted_iota(jnp.int32, (256, 256), 1)
            same = (row // 64) == (col // 64)
            for g in range(4):
                qg, kg, vg = [turned[i, g * 4:(g + 1) * 4].reshape(256, HD) for i in range(3)]
                scores = jnp.where(same, dot(qg, kg, NT) * SCALE, -1e30)
                expo = jnp.exp(scores - jnp.max(scores, axis=1, keepdims=True))
                total = jnp.sum(expo, axis=1, keepdims=True)
                result = dot(expo.astype(BF16), vg) / total
                done[g * 4:(g + 1) * 4] = result.astype(BF16).reshape(4, 64, HD)
            for c in range(4):
                rows = dot(swap, done[:, c * 16:(c + 1) * 16, :].reshape(256, HD))
                back[c * 16:(c + 1) * 16] = rows.astype(BF16).reshape(16, 16, HD)

            def one(i, carry):
                to = (frame + i) % 64
                send(back.at[to], backed.at[half, y * 3 + my_k], b_s, b_r.at[half], frame=to)
                return carry

            lax.fori_loop(1, 64, one, 0)
            backed[half, y * 3 + my_k] = back[frame]

    def w_y1():
        for i in range(1, 6):
            send(wg.at[0, j], wg.at[i, j], wy_s.at[i], wy_r.at[i], frame=at(turn(y, -DY[i], 8), j))

    def w_y2(group):
        first, count = GROUPS[group]
        for i in range(first, first + count):
            wait_for(wg.at[i, j], wy_r.at[i])
            if i in (4, 5):
                to, way = (7, 1) if i == 4 else (6, -1)
                send(wg.at[i, j], wg.at[to, j], wy_s.at[to], wy_r.at[to], frame=at(turn(y, way, 8), j))

    def cut(group, jj):
        first, count = GROUPS[group]
        return wg.at[pl.ds(first, count), jj]

    def w_x1(group):
        src = cut(group, j)
        send(src, src, wx_s.at[0, group], wx_r.at[0, group], frame=at(y, j_right))
        send(src, src, wx_s.at[1, group], wx_r.at[1, group], frame=at(y, j_left))
        send(src, src, wp_s.at[0, group], wp_r.at[0, group], frame=partner)

    def w_x2(group):
        for way, jj in ((1, j_right), (0, j_left)):
            src = cut(group, jj)
            wait_for(src, wx_r.at[way, group])
            if way == ONWARD[group]:
                to = j_left if way == 1 else j_right
                send(src, src, wf_s.at[group], wf_r.at[group], frame=at(y, to))
            send(src, src, wp_s.at[2 - way, group], wp_r.at[2 - way, group], frame=partner)

    def w_x3(group):
        src = cut(group, j_far)
        wait_for(src, wf_r.at[group])
        send(src, src, wp_s.at[3, group], wp_r.at[3, group], frame=partner)

    def w_done(group):
        for i, jj in enumerate((j, j_right, j_left, j_far)):
            wait_for(cut(group, jj + shift), wp_r.at[i, group])

    def spatial():
        pick = one_hot(192, 256, lambda out: ((out % 32) // 4) * 32 + (out // 32) * 4 + out % 4)
        for d in range(8):
            rows = dot(pick, text[d].reshape(256, HD)).astype(BF16)
            toks[:, d * 32:(d + 1) * 32, :] = rows.reshape(6, 32, HD)
        col = lax.broadcasted_iota(jnp.int32, (256, 256), 1)
        live = (y * 32 + col) % 256 < count_ref[0]
        for h in range(3):
            lanes = pl.ds(h * HD, HD)
            qh = qb[:, lanes]
            own = dot(qh, kb[:, lanes], NT) * SCALE
            other = jnp.where(live, dot(qh, toks[h], NT) * SCALE, -1e30)
            top = jnp.maximum(
                jnp.max(own, axis=1, keepdims=True), jnp.max(other, axis=1, keepdims=True)
            )
            e_own = jnp.exp(own - top)
            e_other = jnp.exp(other - top)
            total = jnp.sum(e_own, axis=1, keepdims=True) + jnp.sum(e_other, axis=1, keepdims=True)
            result = dot(e_own.astype(BF16), vb[:, lanes]) + dot(e_other.astype(BF16), toks[3 + h])
            spat[:, :, :, lanes] = (result / total).astype(BF16).reshape(8, 2, 16, HD)

    def length(pair, way):
        return 4 if (pair + way) % 2 == 0 else 3

    def dest(pair, way, stage):
        left = length(pair, way) - stage
        return turn(z, left if way == 0 else -left, 8)

    def pass_on(src, pair, way, stage):
        at_sem = (way, pair, stage)
        send(src, rrecv.at[at_sem], rs_s.at[at_sem], rs_r.at[at_sem], head=turn(z, 1 - 2 * way, 8))

    def mix(half):
        counted(half, backed.at[half], 24, b_r.at[half])
        for h in range(3):
            lanes = pl.ds(h * HD, HD)
            temp = backed[half].reshape(8, 3, 16, HD)[:, h]
            mixed[:, half, :, lanes] = jnp.where(kinds_ref[z * 3 + h] == 1, temp, spat[:, half, :, lanes])

    def project(pair):
        for i in range(2):
            term = dot(mixed[...].reshape(256, 384), wg[pair * 2 + i].reshape(384, 384), NT)
            part[pair, :, i] = term.astype(BF16).reshape(8, 32, 384)
        for way in range(2):
            pass_on(part.at[pair, dest(pair, way, 0)], pair, way, 0)

    def reduce(stage):
        for pair in range(4):
            for way in range(2):
                if stage < length(pair, way):
                    before = (way, pair, stage - 1)
                    now = (way, pair, stage)
                    wait_for(rrecv.at[before], rs_r.at[before])
                    own = part[pair, dest(pair, way, stage)].astype(F32)
                    rsend[now] = (own + rrecv[before].astype(F32)).astype(BF16)
                    pass_on(rsend.at[now], pair, way, stage)

    def finish():
        for pair in range(4):
            own = part[pair, z].astype(F32)
            for way in range(2):
                last = (way, pair, length(pair, way) - 1)
                wait_for(rrecv.at[last], rs_r.at[last])
                own = own + rrecv[last].astype(F32)
            for i in range(2):
                block = turn(y, DY[pair * 2 + i], 8)
                columns = pl.ds(pl.multiple_of(block * 384, 384), 384)
                out_ref[:, columns] = own[i].astype(BF16)

    def drain_rs():
        for pair in range(4):
            for way in range(2):
                for stage in range(length(pair, way)):
                    now = (way, pair, stage)
                    wait_for(rrecv.at[now], rs_s.at[now])

    def drain_text():
        for d in range(1, 8):
            wait_for(text.at[d, j], ty_s.at[d])
        col = text.at[pl.ds(0, 8), j]
        for i in range(3):
            wait_for(col, tx_s.at[i])
        for i in range(4):
            wait_for(col, tp_s.at[i])

    def drain_w():
        for i in range(1, 8):
            wait_for(wg.at[i, j], wy_s.at[i])
        for group in range(5):
            wait_for(cut(group, j), wx_s.at[0, group])
            wait_for(cut(group, j), wx_s.at[1, group])
            wait_for(cut(group, j), wf_s.at[group])
            for i in range(4):
                wait_for(cut(group, j), wp_s.at[i, group])

    def drain_back():
        @pl.when(jnp.logical_or(active[0], active[1]))
        def _():
            wait_for(back.at[pl.ds(0, 63)], b_s)

    w_y1()
    w_x1(0)
    text_y()
    forward(0, 0)
    forward(0, 1)
    forward(0, 2)
    forward(0, 3)
    w_y2(1)
    w_x1(1)
    w_y2(2)
    w_x1(2)
    forward(1, 0)
    forward(1, 1)
    forward(1, 2)
    forward(1, 3)
    w_x2(0)
    w_y2(3)
    w_x1(3)
    text_x()
    temporal(0)
    w_x2(1)
    w_x2(2)
    w_y2(4)
    w_x1(4)
    w_x3(0)
    text_x2()
    w_x2(3)
    w_x3(1)
    w_x3(2)
    w_x2(4)
    temporal(1)
    text_p()
    w_x3(3)
    text_done()
    spatial()
    mix(0)
    w_done(0)
    w_done(1)
    w_x3(4)
    mix(1)
    project(0)
    w_done(2)
    project(1)
    w_done(3)
    project(2)
    w_done(4)
    project(3)
    reduce(1)
    reduce(2)
    reduce(3)
    finish()
    forward_sent(0, 0)
    forward_sent(0, 1)
    forward_sent(0, 2)
    forward_sent(0, 3)
    forward_sent(1, 0)
    forward_sent(1, 1)
    forward_sent(1, 2)
    forward_sent(1, 3)
    drain_rs()
    drain_text()
    drain_w()
    drain_back()


def per_device(queries, keys, values, text_keys, text_values, head_kinds, text_count, w_out):
    anywhere = pl.BlockSpec(memory_space=pl.ANY)
    vmem = pl.BlockSpec(memory_space=pltpu.VMEM)
    smem = pl.BlockSpec(memory_space=pltpu.SMEM)
    dma = pltpu.SemaphoreType.DMA
    return pl.pallas_call(
        kernel,
        out_shape=jax.ShapeDtypeStruct((32, 3072), BF16),
        in_specs=[anywhere] * 6 + [smem] * 2,
        out_specs=vmem,
        scratch_shapes=[
            pltpu.VMEM((256, 384), BF16),
            pltpu.VMEM((256, 384), BF16),
            pltpu.VMEM((256, 384), BF16),
            pltpu.VMEM((4, 384), BF16),
            pltpu.VMEM((4, 384), BF16),
            pltpu.VMEM((2, 8, 3, 48, HD), BF16),
            pltpu.VMEM((64, 48, HD), BF16),
            pltpu.VMEM((3, 16, 64, HD), BF16),
            pltpu.VMEM((16, 64, HD), BF16),
            pltpu.VMEM((64, 16, HD), BF16),
            pltpu.VMEM((2, 24, 16, HD), BF16),
            pltpu.VMEM((8, 8, 48, 384), BF16),
            pltpu.VMEM((32, HD), F32),
            pltpu.VMEM((8, 8, 32, HD), BF16),
            pltpu.VMEM((6, 256, HD), BF16),
            pltpu.VMEM((8, 2, 16, 384), BF16),
            pltpu.VMEM((8, 2, 16, 384), BF16),
            pltpu.VMEM((4, 8, 2, 32, 384), BF16),
            pltpu.VMEM((2, 4, 4, 2, 32, 384), BF16),
            pltpu.VMEM((2, 4, 4, 2, 32, 384), BF16),
            dma((6,)),
            dma((2, 4)),
            dma,
            dma,
            dma((2,)),
            dma((8,)),
            dma((8,)),
            dma((3,)),
            dma((3,)),
            dma((4,)),
            dma((4,)),
            dma((8,)),
            dma((8,)),
            dma((2, 5)),
            dma((2, 5)),
            dma((5,)),
            dma((5,)),
            dma((4, 5)),
            dma((4, 5)),
            dma((2, 4, 4)),
            dma((2, 4, 4)),
        ],
        compiler_params=pltpu.CompilerParams(
            collective_id=0, has_side_effects=True, vmem_limit_bytes=60 * 1024 * 1024
        ),
    )(queries, keys, values, text_keys, text_values, w_out.T, head_kinds, text_count)


def solution(mesh):
    in_specs = (
        P("frame", "head"),
        P("frame", "head"),
        P("frame", "head"),
        P("frame", "head"),
        P("frame", "head"),
        P(),
        P(),
        P("head", "frame"),
    )
    out_specs = P(("frame", "head"), None)
    return jax.shard_map(
        per_device, mesh=mesh, in_specs=in_specs, out_specs=out_specs, check_vma=False
    )
```

```python
import jax
import jax.numpy as jnp
from jax import lax
from jax.experimental import pallas as pl
from jax.experimental.pallas import tpu as pltpu
from jax.sharding import PartitionSpec as P

HD = 128
MESH = pl.DeviceIdType.MESH
F32 = jnp.float32
BF16 = jnp.bfloat16
NT = (((1,), (1,)), ((), ()))
NN = (((1,), (0,)), ((), ()))
SCALE = HD ** (-0.5)
DY = (0, 1, 7, 2, 6, 3, 4, 5)
BATCHES = ((4, 7), (3, 6), (2, 5), (1, 0))
GROUPS = ((0, 1), (1, 2), (3, 2), (5, 1), (6, 2))
ONWARD = (1, 0, 1, 0, 1)
FAR_FIRST = (4, 3, 5, 2, 6, 1, 7)


def dot(a, b, dims=NN):
    return lax.dot_general(a, b, dims, preferred_element_type=F32)


def send(src, dst, send_sem, recv_sem, **where):
    copy = pltpu.make_async_remote_copy(
        src_ref=src, dst_ref=dst, send_sem=send_sem, recv_sem=recv_sem,
        device_id=where, device_id_type=MESH,
    )
    copy.start()


def wait_for(ref, sem):
    pltpu.make_async_copy(ref, ref, sem).wait()


def one_hot(rows, cols, want):
    out = lax.broadcasted_iota(jnp.int32, (rows, cols), 0)
    src = lax.broadcasted_iota(jnp.int32, (rows, cols), 1)
    return jnp.where(src == want(out), 1.0, 0.0).astype(BF16)


def kernel(
    q_hbm, k_hbm, v_hbm, tk_hbm, tv_hbm, w_hbm, kinds_ref, count_ref, out_ref,
    qb, kb, vb, tkb, tvb, pack, got, turned, done, back, backed, wg, text32, text, toks, spat, mixed,
    part, rsend, rrecv,
    in_sem, f_s, f_r, b_s, b_r, ty_s, ty_r, tx_s, tx_r, tp_s, tp_r,
    wy_s, wy_r, wx_s, wx_r, wf_s, wf_r, wp_s, wp_r, rs_s, rs_r,
):
    frame = lax.axis_index("frame")
    z = lax.axis_index("head")
    y = frame // 8
    j = frame % 8
    x = j // 2
    core = j % 2

    def at(yy, jj):
        return yy * 8 + jj

    def turn(base, step, size):
        return (base + step + size) % size

    j_right = turn(x, 1, 4) * 2 + core
    j_left = turn(x, -1, 4) * 2 + core
    j_far = turn(x, 2, 4) * 2 + core
    shift = 1 - 2 * core
    partner = at(y, j + shift)

    barrier = pltpu.get_barrier_semaphore()

    def greet(i, carry):
        pl.semaphore_signal(barrier, inc=1, device_id={"frame": (frame + i) % 64}, device_id_type=MESH)
        return carry

    lax.fori_loop(1, 64, greet, 0)
    for k in (1, -1):
        pl.semaphore_signal(barrier, inc=1, device_id={"head": turn(z, k, 8)}, device_id_type=MESH)

    loads = [
        pltpu.make_async_copy(src, dst, in_sem.at[i])
        for i, (src, dst) in enumerate(
            ((q_hbm, qb), (k_hbm, kb), (v_hbm, vb), (tk_hbm, tkb), (tv_hbm, tvb), (w_hbm, wg.at[0, j]))
        )
    ]
    for load in loads:
        load.start()
    text32[...] = jnp.zeros_like(text32)
    loads[3].wait()
    loads[4].wait()
    for h in range(3):
        lanes = pl.ds(h * HD, HD)
        text32[h * 4:h * 4 + 4, :] = tkb[:, lanes].astype(F32)
        text32[12 + h * 4:16 + h * 4, :] = tvb[:, lanes].astype(F32)
    text[0, j] = text32[...].astype(BF16)
    for i, (load, buf) in enumerate(zip(loads, (qb, kb, vb))):
        load.wait()
        for h in range(3):
            units = buf[:, h * HD:(h + 1) * HD].reshape(8, 2, 16, HD)
            for half in range(2):
                pack[half, :, h, i * 16:(i + 1) * 16, :] = units[:, half]

    loads[5].wait()

    def unit_j(half, yy, k):
        return ((yy + k) % 4) * 2 + half

    my_k = (x - y + 8) % 4
    active = [jnp.logical_and(core == half, my_k < 3) for half in range(2)]

    pl.semaphore_wait(barrier, 65)

    def text_y():
        for d in FAR_FIRST:
            send(text.at[0, j], text.at[d, j], ty_s.at[d], ty_r.at[d], frame=at(turn(y, -d, 8), j))

    def text_x():
        for d in range(1, 8):
            wait_for(text.at[d, j], ty_r.at[d])
        col = text.at[pl.ds(0, 8), j]
        send(col, col, tx_s.at[0], tx_r.at[0], frame=at(y, j_left))
        send(col, col, tx_s.at[1], tx_r.at[1], frame=at(y, j_right))
        send(col, col, tp_s.at[3], tp_r.at[3], frame=partner)

    def text_x2():
        col = text.at[pl.ds(0, 8), j_right]
        wait_for(col, tx_r.at[0])
        send(col, col, tx_s.at[2], tx_r.at[2], frame=at(y, j_left))
        send(col, col, tp_s.at[2], tp_r.at[2], frame=partner)
        col = text.at[pl.ds(0, 8), j_left]
        wait_for(col, tx_r.at[1])
        send(col, col, tp_s.at[1], tp_r.at[1], frame=partner)

    def text_p():
        col = text.at[pl.ds(0, 8), j_far]
        wait_for(col, tx_r.at[2])
        send(col, col, tp_s.at[0], tp_r.at[0], frame=partner)

    def text_done():
        for i, jj in enumerate((j_far, j_left, j_right, j)):
            wait_for(text.at[pl.ds(0, 8), jj + shift], tp_r.at[i])

    def forward(half, batch):
        for d in BATCHES[batch]:
            yy = turn(y, d, 8)
            for k in range(3):
                jj = unit_j(half, yy, k)

                def one():
                    send(pack.at[half, yy, k], got.at[frame], f_s.at[half, batch], f_r, frame=at(yy, jj))

                if d == 0:
                    pl.when(j != jj)(one)
                else:
                    one()
        if 0 in BATCHES[batch]:
            @pl.when(active[half])
            def _():
                got[frame] = pack[half, y, my_k]

    def counted(half, ref, count, sem):
        @pl.when(active[half])
        def _():
            wait_for(ref.at[pl.ds(0, count - 1)], sem)

        @pl.when(jnp.logical_not(active[half]))
        def _():
            wait_for(ref.at[pl.ds(0, count)], sem)

    def forward_sent(half, batch):
        if 0 in BATCHES[batch]:
            counted(half, got, 6, f_s.at[half, batch])
        else:
            wait_for(got.at[pl.ds(0, 6)], f_s.at[half, batch])

    def temporal(half):
        @pl.when(active[half])
        def _():
            wait_for(got.at[pl.ds(0, 63)], f_r)
            swap = one_hot(256, 256, lambda out: (out % 16) * 16 + out // 16)
            for c in range(4):
                rows = jnp.concatenate(
                    [got[c * 16:(c + 1) * 16, i * 16:(i + 1) * 16, :].reshape(256, HD) for i in range(3)],
                    axis=1,
                )
                rows = dot(swap, rows).astype(BF16)
                for i in range(3):
                    turned[i, :, c * 16:(c + 1) * 16, :] = rows[:, i * HD:(i + 1) * HD].reshape(16, 16, HD)
            row = lax.broadcasted_iota(jnp.int32, (256, 256), 0)
            col = lax.broadcasted_iota(jnp.int32, (256, 256), 1)
            same = (row // 64) == (col // 64)
            for g in range(4):
                qg, kg, vg = [turned[i, g * 4:(g + 1) * 4].reshape(256, HD) for i in range(3)]
                scores = jnp.where(same, dot(qg, kg, NT) * SCALE, -1e30)
                expo = jnp.exp(scores - jnp.max(scores, axis=1, keepdims=True))
                total = jnp.sum(expo, axis=1, keepdims=True)
                result = dot(expo.astype(BF16), vg) / total
                done[g * 4:(g + 1) * 4] = result.astype(BF16).reshape(4, 64, HD)
            for c in range(4):
                rows = dot(swap, done[:, c * 16:(c + 1) * 16, :].reshape(256, HD))
                back[c * 16:(c + 1) * 16] = rows.astype(BF16).reshape(16, 16, HD)

            def one(i, carry):
                to = (frame + i) % 64
                send(back.at[to], backed.at[half, y * 3 + my_k], b_s, b_r.at[half], frame=to)
                return carry

            lax.fori_loop(1, 64, one, 0)
            backed[half, y * 3 + my_k] = back[frame]

    def w_y1():
        for i in range(1, 6):
            send(wg.at[0, j], wg.at[i, j], wy_s.at[i], wy_r.at[i], frame=at(turn(y, -DY[i], 8), j))

    def w_y2(group):
        first, count = GROUPS[group]
        for i in range(first, first + count):
            wait_for(wg.at[i, j], wy_r.at[i])
            if i in (4, 5):
                to, way = (7, 1) if i == 4 else (6, -1)
                send(wg.at[i, j], wg.at[to, j], wy_s.at[to], wy_r.at[to], frame=at(turn(y, way, 8), j))

    def cut(group, jj):
        first, count = GROUPS[group]
        return wg.at[pl.ds(first, count), jj]

    def w_x1(group):
        src = cut(group, j)
        send(src, src, wx_s.at[0, group], wx_r.at[0, group], frame=at(y, j_right))
        send(src, src, wx_s.at[1, group], wx_r.at[1, group], frame=at(y, j_left))
        send(src, src, wp_s.at[0, group], wp_r.at[0, group], frame=partner)

    def w_x2(group):
        for way, jj in ((1, j_right), (0, j_left)):
            src = cut(group, jj)
            wait_for(src, wx_r.at[way, group])
            if way == ONWARD[group]:
                to = j_left if way == 1 else j_right
                send(src, src, wf_s.at[group], wf_r.at[group], frame=at(y, to))
            send(src, src, wp_s.at[2 - way, group], wp_r.at[2 - way, group], frame=partner)

    def w_x3(group):
        src = cut(group, j_far)
        wait_for(src, wf_r.at[group])
        send(src, src, wp_s.at[3, group], wp_r.at[3, group], frame=partner)

    def w_done(group):
        for i, jj in enumerate((j, j_right, j_left, j_far)):
            wait_for(cut(group, jj + shift), wp_r.at[i, group])

    def spatial():
        pick = one_hot(192, 256, lambda out: ((out % 32) // 4) * 32 + (out // 32) * 4 + out % 4)
        for d in range(8):
            rows = dot(pick, text[d].reshape(256, HD)).astype(BF16)
            toks[:, d * 32:(d + 1) * 32, :] = rows.reshape(6, 32, HD)
        col = lax.broadcasted_iota(jnp.int32, (256, 256), 1)
        live = (y * 32 + col) % 256 < count_ref[0]
        for h in range(3):
            lanes = pl.ds(h * HD, HD)
            qh = qb[:, lanes]
            own = dot(qh, kb[:, lanes], NT) * SCALE
            other = jnp.where(live, dot(qh, toks[h], NT) * SCALE, -1e30)
            top = jnp.maximum(
                jnp.max(own, axis=1, keepdims=True), jnp.max(other, axis=1, keepdims=True)
            )
            e_own = jnp.exp(own - top)
            e_other = jnp.exp(other - top)
            total = jnp.sum(e_own, axis=1, keepdims=True) + jnp.sum(e_other, axis=1, keepdims=True)
            result = dot(e_own.astype(BF16), vb[:, lanes]) + dot(e_other.astype(BF16), toks[3 + h])
            spat[:, :, :, lanes] = (result / total).astype(BF16).reshape(8, 2, 16, HD)

    def length(pair, way):
        return 4 if (pair + way) % 2 == 0 else 3

    def dest(pair, way, stage):
        left = length(pair, way) - stage
        return turn(z, left if way == 0 else -left, 8)

    def pass_on(src, half, pair, way, stage):
        at_sem = (half, way, pair, stage)
        send(src, rrecv.at[at_sem], rs_s.at[at_sem], rs_r.at[at_sem], head=turn(z, 1 - 2 * way, 8))

    def mix(half):
        counted(half, backed.at[half], 24, b_r.at[half])
        for h in range(3):
            lanes = pl.ds(h * HD, HD)
            temp = backed[half].reshape(8, 3, 16, HD)[:, h].reshape(128, HD)
            own = spat[:, half, :, lanes].reshape(128, HD)
            mixed[half, :, lanes] = jnp.where(kinds_ref[z * 3 + h] == 1, temp, own)

    def project(half, pair):
        for i in range(2):
            term = dot(mixed[half], wg[pair * 2 + i].reshape(384, 384), NT)
            part[half, pair, :, i] = term.astype(BF16).reshape(8, 16, 384)
        for way in range(2):
            pass_on(part.at[half, pair, dest(pair, way, 0)], half, pair, way, 0)

    def reduce(half, stage):
        for pair in range(4):
            for way in range(2):
                if stage < length(pair, way):
                    before = (half, way, pair, stage - 1)
                    now = (half, way, pair, stage)
                    wait_for(rrecv.at[before], rs_r.at[before])
                    own = part[half, pair, dest(pair, way, stage)].astype(F32)
                    rsend[now] = (own + rrecv[before].astype(F32)).astype(BF16)
                    pass_on(rsend.at[now], half, pair, way, stage)

    def finish(half):
        for pair in range(4):
            own = part[half, pair, z].astype(F32)
            for way in range(2):
                last = (half, way, pair, length(pair, way) - 1)
                wait_for(rrecv.at[last], rs_r.at[last])
                own = own + rrecv[last].astype(F32)
            for i in range(2):
                block = turn(y, DY[pair * 2 + i], 8)
                columns = pl.ds(pl.multiple_of(block * 384, 384), 384)
                out_ref[half * 16:(half + 1) * 16, columns] = own[i].astype(BF16)

    def drain_rs(half):
        for pair in range(4):
            for way in range(2):
                for stage in range(length(pair, way)):
                    now = (half, way, pair, stage)
                    wait_for(rrecv.at[now], rs_s.at[now])

    def drain_text():
        for d in range(1, 8):
            wait_for(text.at[d, j], ty_s.at[d])
        col = text.at[pl.ds(0, 8), j]
        for i in range(3):
            wait_for(col, tx_s.at[i])
        for i in range(4):
            wait_for(col, tp_s.at[i])

    def drain_w():
        for i in range(1, 8):
            wait_for(wg.at[i, j], wy_s.at[i])
        for group in range(5):
            wait_for(cut(group, j), wx_s.at[0, group])
            wait_for(cut(group, j), wx_s.at[1, group])
            wait_for(cut(group, j), wf_s.at[group])
            for i in range(4):
                wait_for(cut(group, j), wp_s.at[i, group])

    def drain_back():
        @pl.when(jnp.logical_or(active[0], active[1]))
        def _():
            wait_for(back.at[pl.ds(0, 63)], b_s)

    w_y1()
    w_x1(0)
    text_y()
    forward(0, 0)
    forward(0, 1)
    forward(0, 2)
    forward(0, 3)
    w_y2(1)
    w_x1(1)
    w_y2(2)
    w_x1(2)
    forward(1, 0)
    forward(1, 1)
    forward(1, 2)
    forward(1, 3)
    w_x2(0)
    w_y2(3)
    w_x1(3)
    text_x()
    temporal(0)
    w_x2(1)
    w_x2(2)
    w_y2(4)
    w_x1(4)
    w_x3(0)
    text_x2()
    w_x2(3)
    w_x3(1)
    w_x3(2)
    w_x2(4)
    temporal(1)
    text_p()
    w_x3(3)
    text_done()
    spatial()
    w_done(0)
    w_done(1)
    mix(0)
    project(0, 0)
    w_x3(4)
    w_done(2)
    project(0, 1)
    w_done(3)
    project(0, 2)
    mix(1)
    project(1, 0)
    project(1, 1)
    project(1, 2)
    w_done(4)
    project(0, 3)
    project(1, 3)
    reduce(0, 1)
    reduce(1, 1)
    reduce(0, 2)
    reduce(1, 2)
    reduce(0, 3)
    reduce(1, 3)
    finish(0)
    finish(1)
    forward_sent(0, 0)
    forward_sent(0, 1)
    forward_sent(0, 2)
    forward_sent(0, 3)
    forward_sent(1, 0)
    forward_sent(1, 1)
    forward_sent(1, 2)
    forward_sent(1, 3)
    drain_rs(0)
    drain_rs(1)
    drain_text()
    drain_w()
    drain_back()


def per_device(queries, keys, values, text_keys, text_values, head_kinds, text_count, w_out):
    anywhere = pl.BlockSpec(memory_space=pl.ANY)
    vmem = pl.BlockSpec(memory_space=pltpu.VMEM)
    smem = pl.BlockSpec(memory_space=pltpu.SMEM)
    dma = pltpu.SemaphoreType.DMA
    return pl.pallas_call(
        kernel,
        out_shape=jax.ShapeDtypeStruct((32, 3072), BF16),
        in_specs=[anywhere] * 6 + [smem] * 2,
        out_specs=vmem,
        scratch_shapes=[
            pltpu.VMEM((256, 384), BF16),
            pltpu.VMEM((256, 384), BF16),
            pltpu.VMEM((256, 384), BF16),
            pltpu.VMEM((4, 384), BF16),
            pltpu.VMEM((4, 384), BF16),
            pltpu.VMEM((2, 8, 3, 48, HD), BF16),
            pltpu.VMEM((64, 48, HD), BF16),
            pltpu.VMEM((3, 16, 64, HD), BF16),
            pltpu.VMEM((16, 64, HD), BF16),
            pltpu.VMEM((64, 16, HD), BF16),
            pltpu.VMEM((2, 24, 16, HD), BF16),
            pltpu.VMEM((8, 8, 48, 384), BF16),
            pltpu.VMEM((32, HD), F32),
            pltpu.VMEM((8, 8, 32, HD), BF16),
            pltpu.VMEM((6, 256, HD), BF16),
            pltpu.VMEM((8, 2, 16, 384), BF16),
            pltpu.VMEM((2, 128, 384), BF16),
            pltpu.VMEM((2, 4, 8, 2, 16, 384), BF16),
            pltpu.VMEM((2, 2, 4, 4, 2, 16, 384), BF16),
            pltpu.VMEM((2, 2, 4, 4, 2, 16, 384), BF16),
            dma((6,)),
            dma((2, 4)),
            dma,
            dma,
            dma((2,)),
            dma((8,)),
            dma((8,)),
            dma((3,)),
            dma((3,)),
            dma((4,)),
            dma((4,)),
            dma((8,)),
            dma((8,)),
            dma((2, 5)),
            dma((2, 5)),
            dma((5,)),
            dma((5,)),
            dma((4, 5)),
            dma((4, 5)),
            dma((2, 2, 4, 4)),
            dma((2, 2, 4, 4)),
        ],
        compiler_params=pltpu.CompilerParams(
            collective_id=0, has_side_effects=True, vmem_limit_bytes=60 * 1024 * 1024
        ),
    )(queries, keys, values, text_keys, text_values, w_out.T, head_kinds, text_count)


def solution(mesh):
    in_specs = (
        P("frame", "head"),
        P("frame", "head"),
        P("frame", "head"),
        P("frame", "head"),
        P("frame", "head"),
        P(),
        P(),
        P("head", "frame"),
    )
    out_specs = P(("frame", "head"), None)
    return jax.shard_map(
        per_device, mesh=mesh, in_specs=in_specs, out_specs=out_specs, check_vma=False
    )
```
